512 devices in a mesh: sec: 8 (over y_hi, x), space: 64 (over z, y_lo, core).
Axes of the slice: x: 4, y: 8 (y_hi: 2, y_lo: 4; y = y_hi * 4 + y_lo), z: 8, core: 2. Of those that a mesh axis runs over, the one named last changes fastest.
Arguments:
- density: float32 [64, 256, 64, 128], P('sec', 'space'), may hold values from 0.1 to 2
- wind_speed: float32 [256, 64, 128], P('space'), may hold values from -0.35 to 0.35
- settling: float32 [64], P('sec'), may hold values from 0.05 to 0.25
- diffusion: float32 [64], P('sec'), may hold values from 0.01 to 0.06
- breakup: bfloat16 [64, 64], replicated, may hold values from -0.375 to 0.375
- coag_kernel: float32 [64, 64], replicated, may hold values from 0.0025 to 0.02
- pair_target: int32 [64, 64], replicated, may hold values from 0 to 63, as said below
Outputs:
- updated: float32 [64, 256, 64, 128], P('sec', 'space')
The draws below stay inside these ranges and needn't reach their ends.
Inputs may be any that keep to these rules, and one draw needn't show every extreme that they name: pair_target[i,j] is at least the larger of i and j.
All inputs are finite; a program needn't handle non-finite values.
Results may differ from the reference program's by a relative error of at most 0.0012.
Values may be sent and summed in bfloat16 or wider, within the bound.
No kernel may reach another device: no remote copies, remote signals or barrier semaphores. Data moves between devices by JAX's collectives and lax.ppermute only.
A program may use at most 64 MiB of HBM per device.

```python
import math
import jax
import jax.numpy as jnp
from jax import lax

S = 64
NY = 64
NZ = 128
SUBSTEPS = 2
NX = 256


def draw_pair_target(key, part):
    key = jax.random.fold_in(key, 7)
    extra = jax.random.randint(key, (S, S), 0, 3)
    rows = jnp.arange(S, dtype=jnp.int32)
    larger = jnp.maximum(rows[:, None], rows[None, :])
    return jnp.minimum(larger + extra, S - 1).astype(jnp.int32)


def block_levels(key, dims, split, low, largest):
    loudness, own = 1.0, jax.random.fold_in(key, 6)
    for dim, blocks in split:
        draws = jnp.exp(jax.random.uniform(jax.random.fold_in(own, dim), (blocks,), jnp.float32, low / len(split), largest / len(split)))
        loudness = loudness * jnp.repeat(draws, dims[dim] // blocks).reshape([-1 if axis == dim else 1 for axis in range(len(dims))])
    return loudness


def centred(key, dims, scale, most, held_as=jnp.bfloat16):
    return jnp.clip(scale * jax.random.normal(key, dims, jnp.float32), -most, most).astype(held_as)


def setup_inputs(seed: int = 0) -> dict:
    seeds = jax.random.split(jax.random.key(seed), 8)
    return {
        "density": jnp.clip(jnp.exp(math.log(2.0) - 2.9957323 * jax.random.uniform(seeds[0], (S, NX, NY, NZ), jnp.float32) ** block_levels(seeds[0], (S, NX, NY, NZ), ((0, 8), (1, 64)), -0.2, 0.2)), 0.1, 2.0),
        "wind_speed": jnp.clip(jax.random.uniform(seeds[1], (NX, NY, NZ), jnp.float32, -0.35, 0.35) * block_levels(seeds[1], (NX, NY, NZ), ((0, 64),), -0.4, 0.0), -0.35, 0.35),
        "settling": jnp.clip(jnp.exp(math.log(0.25) - 1.609438 * jax.random.uniform(seeds[2], (S,), jnp.float32) ** block_levels(seeds[2], (S,), ((0, 8),), -0.2, 0.2)), 0.05, 0.25),
        "diffusion": jnp.clip(jnp.exp(math.log(0.06) - 1.7917595 * jax.random.uniform(seeds[3], (S,), jnp.float32) ** block_levels(seeds[3], (S,), ((0, 8),), -0.2, 0.2)), 0.01, 0.06),
        "breakup": centred(seeds[4], (S, S), (4 * S) ** -0.5, 0.375),
        "coag_kernel": jnp.clip(jnp.exp(jax.random.uniform(seeds[5], (S, S), jnp.float32, math.log(0.0025), math.log(0.02))), 0.0025, 0.02),
        "pair_target": draw_pair_target(jax.random.fold_in(seeds[7], 71), 0),
    }


def substep(field, wind_speed, settling, diffusion):
    padded = jnp.pad(field, ((0, 0), (1, 1), (1, 1), (1, 1)))
    center = padded[:, 1:-1, 1:-1, 1:-1]
    west_cell = padded[:, :-2, 1:-1, 1:-1]
    east_cell = padded[:, 2:, 1:-1, 1:-1]
    north_cell = padded[:, 1:-1, 2:, 1:-1]
    south_cell = padded[:, 1:-1, :-2, 1:-1]
    above_cell = padded[:, 1:-1, 1:-1, 2:]
    below_cell = padded[:, 1:-1, 1:-1, :-2]
    forward = jnp.maximum(wind_speed, 0.0)
    backward = jnp.minimum(wind_speed, 0.0)
    advected = forward * (center - west_cell) + backward * (east_cell - center)
    settled = settling[:, None, None, None] * (above_cell - center)
    laplace = west_cell + east_cell + north_cell + south_cell + above_cell + below_cell - 6.0 * center
    return center - advected + settled + diffusion[:, None, None, None] * laplace


def kinetics(cells_block, breakup, kernel_bf, pair_table):
    sections = cells_block.shape[0]
    fragments = jnp.dot(breakup, cells_block, preferred_element_type=jnp.float32)
    loss_rate = jnp.dot(kernel_bf, cells_block, preferred_element_type=jnp.float32)
    pair_sums = jnp.dot(pair_table, cells_block, preferred_element_type=jnp.float32)
    pair_sums = pair_sums.reshape(sections, sections, -1)
    as_float = cells_block.astype(jnp.float32)
    gained = jnp.sum(as_float[:, None, :] * pair_sums, axis=0)
    return (fragments + gained - as_float * loss_rate).astype(jnp.bfloat16)


def reference(density, wind_speed, settling, diffusion, breakup, coag_kernel, pair_target):
    field = density
    for step_index in range(SUBSTEPS):
        field = substep(field, wind_speed, settling, diffusion)
    sections = field.shape[0]
    rounded = field.astype(jnp.bfloat16).reshape(sections, -1)
    targets = jnp.arange(sections, dtype=jnp.int32)
    onehot = (pair_target[:, :, None] == targets[None, None, :]).astype(jnp.float32)
    pair_table = jnp.transpose(coag_kernel[:, :, None] * onehot, (0, 2, 1)).reshape(sections * sections, sections).astype(jnp.bfloat16)
    kernel_bf = coag_kernel.astype(jnp.bfloat16)
    total_cells = rounded.shape[1]
    block_size = 4096
    blocks = rounded.reshape(sections, total_cells // block_size, block_size)
    blocks = jnp.transpose(blocks, (1, 0, 2))
    tendency = lax.map(lambda cells_block: kinetics(cells_block, breakup, kernel_bf, pair_table), blocks)
    tendency = jnp.transpose(tendency, (1, 0, 2)).reshape(field.shape)
    return field + 0.25 * tendency.astype(jnp.float32)
```

```python
import functools

import jax
import jax.numpy as jnp
from jax import lax
from jax.experimental import pallas as pl
from jax.experimental.pallas import tpu as pltpu
from jax.sharding import PartitionSpec as P

BF = jnp.bfloat16
F32 = jnp.float32
S = 64
OWN = 8
LAYERS = 4
NY = 64
NZ = 128
HALF = 32
PAIRS = HALF // 2
STEP = 0.25
TABLE_ROWS = 2 * S + sum(8 * (S - 8 * g) for g in range(8))
LIMIT = 48 * 1024 * 1024


def call(body, out_shape, scratch=(), in_specs=None):
    more = {} if in_specs is None else {"in_specs": in_specs}
    return pl.pallas_call(
        body,
        out_shape=out_shape,
        scratch_shapes=scratch,
        compiler_params=pltpu.CompilerParams(vmem_limit_bytes=LIMIT),
        **more,
    )


def strided(x, y):
    return pl.ds(x * NY + y, OWN, stride=LAYERS * NY)


def pack_body(density, wind, low, high):
    def rows(p, _):
        for out, first in ((low, 0), (high, 2)):
            for l in range(2):
                a = density[strided(first + l, 2 * p), :]
                b = density[strided(first + l, 2 * p + 1), :]
                out[l * HALF + p] = jnp.concatenate([a, b], 0).astype(BF)
        return 0

    lax.fori_loop(0, HALF, rows, 0, unroll=4)
    for out, layer in ((low, 0), (high, 3)):
        for t in range(NY // 16):
            out[2 * HALF + t] = wind[layer * NY + 16 * t : layer * NY + 16 * t + 16, :].astype(BF)


def table_body(kernel, target, breakup, table):
    table[0:S, :] = breakup[...]
    table[S : 2 * S, :] = kernel[...].astype(BF)
    base = 2 * S
    for g in range(8):
        low = 8 * g
        count = S - low
        ks = lax.broadcasted_iota(jnp.int32, (count, S), 0) + low
        for i in range(low, low + 8, 2):
            both = [
                jnp.where(target[r : r + 1, :] == ks, kernel[r : r + 1, :], 0.0)
                for r in (i, i + 1)
            ]
            table[base : base + 2 * count, :] = jnp.concatenate(both, 0).astype(BF)
            base += 2 * count


def transport_body(
    inside, density, from_west, from_east, wind, settling, diffusion, field, rounded, old, mid, winds
):
    zero = jnp.zeros((1, OWN, NZ), F32)
    for x in range(LAYERS + 4):
        old[x, 0:1] = zero
        old[x, NY + 1 : NY + 2] = zero
    for x in range(LAYERS + 2):
        mid[x, 0:1] = zero
        mid[x, NY + 1 : NY + 2] = zero

    def bring(p, _):
        for l in range(2):
            for halo, x in ((from_west, l), (from_east, LAYERS + 2 + l)):
                two = halo[l * HALF + p].astype(F32)
                old[x, 2 * p + 1] = two[0:8]
                old[x, 2 * p + 2] = two[8:16]
        for x in range(LAYERS):
            old[x + 2, 2 * p + 1] = density[strided(x, 2 * p), :]
            old[x + 2, 2 * p + 2] = density[strided(x, 2 * p + 1), :]
        return 0

    lax.fori_loop(0, HALF, bring, 0, unroll=2)
    winds[NY : NY + LAYERS * NY, :] = wind[...]
    for t in range(NY // 16):
        winds[16 * t : 16 * t + 16, :] = from_west[2 * HALF + t].astype(F32)
        top = (LAYERS + 1) * NY + 16 * t
        winds[top : top + 16, :] = from_east[2 * HALF + t].astype(F32)

    lane = lax.broadcasted_iota(jnp.int32, (OWN, NZ), 1)
    sink = jnp.broadcast_to(settling[...], (OWN, NZ))
    spread = jnp.broadcast_to(diffusion[...], (OWN, NZ))
    here = 1.0 - sink - 6.0 * spread
    from_above = jnp.where(lane == NZ - 1, 0.0, sink + spread)
    from_below = jnp.where(lane == 0, 0.0, spread)

    def update(ref, x, wind_x, y):
        ten = ref[x, pl.ds(y, 10)]
        c = ten[1:9]
        w = ref[x - 1, pl.ds(y + 1, 8)]
        e = ref[x + 1, pl.ds(y + 1, 8)]
        u = winds[pl.ds(wind_x * NY + y, 8), :]
        u = jnp.broadcast_to(u[:, None, :], (8, OWN, NZ))
        forward = jnp.maximum(u, 0.0)
        backward = jnp.minimum(u, 0.0)
        above = pltpu.roll(c, NZ - 1, 2)
        below = pltpu.roll(c, 1, 2)
        return (
            c * (here - jnp.abs(u))
            + w * (spread + forward)
            + e * (spread - backward)
            + above * from_above
            + below * from_below
            + (ten[0:8] + ten[2:10]) * spread
        )

    def first(b, _):
        y = 8 * b
        for x in range(LAYERS + 2):
            value = update(old, x + 1, x, y)
            if x == 0:
                value = value * inside[0]
            if x == LAYERS + 1:
                value = value * inside[1]
            mid[x, pl.ds(y + 1, 8)] = value
        return 0

    lax.fori_loop(0, NY // 8, first, 0)

    def second(b, _):
        y = 8 * b
        for x in range(LAYERS):
            value = update(mid, x + 1, x + 1, y)
            field[x, pl.ds(y, 8)] = value
            for h in range(4):
                two = jnp.concatenate([value[2 * h], value[2 * h + 1]], 0)
                at = 4 * b + h
                rounded[2 * x + at // PAIRS, lax.rem(at, PAIRS)] = two.astype(BF)
        return 0

    lax.fori_loop(0, NY // 8, second, 0)


def kinetics_body(cells, table, out, wide):
    groups = 2

    def step(q, _):
        parts = []
        for u in range(groups):
            x = cells[:, groups * q + u].astype(F32)
            parts += [x[:, 0:8, :].reshape(S, NZ), x[:, 8:16, :].reshape(S, NZ)]
        n = jnp.concatenate(parts, 1)
        n_bf = n.astype(BF)
        wide[...] = n

        def product(start, stop):
            return jnp.dot(table[start:stop, :], n_bf, preferred_element_type=F32)

        linear = product(0, 2 * S)
        total = linear[0:S] - n * linear[S : 2 * S]
        totals = [total[8 * h : 8 * h + 8] for h in range(8)]
        base = 2 * S
        for g in range(8):
            count = S - 8 * g
            for i in range(8 * g, 8 * g + 8, 2):
                sums = product(base, base + 2 * count)
                base += 2 * count
                at = 0
                for r in (i, i + 1):
                    n_r = wide[r : r + 1, :]
                    for h in range(g, 8):
                        totals[h] = totals[h] + n_r * sums[at : at + 8]
                        at += 8
        total = jnp.concatenate(totals, 0)
        for u in range(groups):
            at = 2 * NZ * u
            a = total[:, at : at + NZ].reshape(8, OWN, NZ)
            b = total[:, at + NZ : at + 2 * NZ].reshape(8, OWN, NZ)
            out[:, groups * q + u] = jnp.concatenate([a, b], 1).astype(BF)
        return 0

    lax.fori_loop(0, PAIRS // groups, step, 0)


def finish_body(field, tendency, out):
    def rows(p, _):
        for x in range(LAYERS):
            for half in range(2):
                y = half * HALF + 2 * p
                two = STEP * tendency[2 * x + half, p].astype(F32)
                out[strided(x, y), :] = field[x, y] + two[0:8]
                out[strided(x, y + 1), :] = field[x, y + 1] + two[8:16]
        return 0

    lax.fori_loop(0, PAIRS, rows, 0, unroll=2)


def per_device(density, wind_speed, settling, diffusion, breakup, coag_kernel, pair_target):
    slabs = lax.axis_size("space")
    me = lax.axis_index("space")
    density = density.reshape(OWN * LAYERS * NY, NZ)
    wind = wind_speed.reshape(LAYERS * NY, NZ)
    forward = [(i, i + 1) for i in range(slabs - 1)]
    backward = [(b, a) for a, b in forward]
    message = jax.ShapeDtypeStruct((2 * HALF + NY // 16, 16, NZ), BF)
    low, high = call(pack_body, (message, message))(density, wind)
    from_west = lax.ppermute(high, "space", forward)
    from_east = lax.ppermute(low, "space", backward)
    table = call(table_body, jax.ShapeDtypeStruct((TABLE_ROWS, S), BF))(
        coag_kernel, pair_target, breakup
    )
    inside = jnp.stack([me > 0, me < slabs - 1]).astype(F32)
    vmem = pl.BlockSpec(memory_space=pltpu.VMEM)
    block = jax.ShapeDtypeStruct((8, PAIRS, 16, NZ), BF)
    field, rounded = call(
        transport_body,
        (jax.ShapeDtypeStruct((LAYERS, NY, OWN, NZ), F32), block),
        scratch=(
            pltpu.VMEM((LAYERS + 4, NY + 2, OWN, NZ), F32),
            pltpu.VMEM((LAYERS + 2, NY + 2, OWN, NZ), F32),
            pltpu.VMEM(((LAYERS + 2) * NY, NZ), F32),
        ),
        in_specs=[pl.BlockSpec(memory_space=pltpu.SMEM)] + [vmem] * 6,
    )(
        inside, density, from_west, from_east, wind,
        settling.reshape(OWN, 1), diffusion.reshape(OWN, 1),
    )
    cells = lax.all_to_all(rounded, "sec", split_axis=0, concat_axis=0, tiled=True)
    tendency = call(kinetics_body, block, scratch=(pltpu.VMEM((S, 4 * NZ), F32),))(cells, table)
    returned = lax.all_to_all(tendency, "sec", split_axis=0, concat_axis=0, tiled=True)
    out = call(finish_body, jax.ShapeDtypeStruct((OWN * LAYERS * NY, NZ), F32))(field, returned)
    return out.reshape(OWN, LAYERS, NY, NZ)


def solution(mesh):
    in_specs = (
        P("sec", "space", None, None),
        P("space", None, None),
        P("sec"),
        P("sec"),
        P(),
        P(),
        P(),
    )
    out_specs = P("sec", "space", None, None)
    return jax.shard_map(
        per_device, mesh=mesh, in_specs=in_specs, out_specs=out_specs, check_vma=False
    )
```

```python
import jax
import jax.numpy as jnp
from jax import lax
from jax.experimental import pallas as pl
from jax.experimental.pallas import tpu as pltpu
from jax.sharding import PartitionSpec as P

BF = jnp.bfloat16
F32 = jnp.float32
S = 64
OWN = 8
LAYERS = 4
NY = 64
NZ = 128
HALF = 32
PAIRS = HALF // 2
STEP = 0.25
PAIR_ROWS = sum(8 * (S - 8 * g) for g in range(8))
LIMIT = 48 * 1024 * 1024


def call(body, out_shape, scratch=(), **specs):
    return pl.pallas_call(
        body,
        out_shape=out_shape,
        scratch_shapes=scratch,
        compiler_params=pltpu.CompilerParams(vmem_limit_bytes=LIMIT),
        **specs,
    )


def bring_layer(loaded, out, x):
    zero = jnp.zeros((1, OWN, NZ), F32)
    out[x, 0:1] = zero
    out[x, NY + 1 : NY + 2] = zero

    def rows(p, _):
        for r in range(8):
            out[x, 8 * p + r + 1] = loaded[pl.ds(8 * p + r, OWN, stride=NY), :]
        return 0

    lax.fori_loop(0, NY // 8, rows, 0, unroll=True)


def pack_layer(layer, x, out, at):
    def rows(p, _):
        for r in range(4):
            two = layer[x, pl.ds(8 * p + 2 * r + 1, 2)].reshape(16, NZ)
            out[at + 4 * p + r] = two.astype(BF)
        return 0

    lax.fori_loop(0, NY // 8, rows, 0, unroll=True)


def pack_body(flags, density, wind, out, old, loaded, windy, sems):
    base = flags[0]
    copies = [
        pltpu.make_async_copy(density.at[:, base], loaded.at[0], sems.at[0]),
        pltpu.make_async_copy(density.at[:, base + 1], loaded.at[1], sems.at[1]),
        pltpu.make_async_copy(wind.at[flags[1]], windy, sems.at[2]),
    ]
    for copy in copies:
        copy.start()
    for l in range(2):
        copies[l].wait()
        bring_layer(loaded.at[l].reshape(OWN * NY, NZ), old, l)
        pack_layer(old, l, out, l * HALF)
    copies[2].wait()
    for t in range(NY // 16):
        out[2 * HALF + t] = windy[16 * t : 16 * t + 16, :].astype(BF)


def table_body(kernel, target, breakup, linear, pairs, columns):
    linear[0:S, :] = breakup[...]
    linear[S : 2 * S, :] = kernel[...].astype(BF)
    rates = kernel[...].astype(BF).astype(F32)
    rates_t = jnp.transpose(rates)
    target_t = jnp.transpose(target[...])
    base = 0
    for g in range(8):
        low = 8 * g
        count = S - low
        ks = lax.broadcasted_iota(jnp.int32, (count, S), 1)
        js = lax.broadcasted_iota(jnp.int32, (count, S), 0) + low
        for i in range(low, low + 8):
            one = jnp.where((target_t[low:, i : i + 1] == ks) & (js >= i), rates_t[low:, i : i + 1], 0.0)
            two = jnp.where((target[low:, i : i + 1] == ks) & (js > i), rates[low:, i : i + 1], 0.0)
            columns[base : base + count, 0:S] = one + two
            base += count
    for t in range(PAIR_ROWS // NZ):
        pairs[:, t * NZ : (t + 1) * NZ] = jnp.transpose(columns[t * NZ : (t + 1) * NZ, :])[0:S, :].astype(BF)


def spread_rows(rows):
    return jnp.broadcast_to(rows[:, None, :], (8, OWN, NZ))


def within(ten, u, constants):
    here, from_above, from_below, spread = constants
    c = ten[1:9]
    return (
        c * (here - jnp.abs(u))
        + pltpu.roll(c, NZ - 1, 2) * from_above
        + pltpu.roll(c, 1, 2) * from_below
        + (ten[0:8] + ten[2:10]) * spread
    )


def from_west_of(u, spread):
    return spread + jnp.maximum(u, 0.0)


def from_east_of(u, spread):
    return spread - jnp.minimum(u, 0.0)


def per_section(ref):
    row = lax.broadcasted_iota(jnp.int32, (OWN, NZ), 0)
    out = jnp.zeros((OWN, NZ), F32)
    for s in range(OWN):
        out = jnp.where(row == s, ref[s], out)
    return out


def inner_body(
    flags, settling, diffusion, sent, kept, wind, kernel, target, breakup,
    old, field, reach, constants, linear, pairs, mid, columns,
):
    table_body(kernel, target, breakup, linear, pairs, columns)
    sink, spread = per_section(settling), per_section(diffusion)
    lane = lax.broadcasted_iota(jnp.int32, (OWN, NZ), 1)
    held = (
        1.0 - sink - 6.0 * spread,
        jnp.where(lane == NZ - 1, 0.0, sink + spread),
        jnp.where(lane == 0, 0.0, spread),
        spread,
    )
    for i in range(4):
        constants[i] = held[i]
    zero = jnp.zeros((1, OWN, NZ), F32)
    for x in range(LAYERS):
        mid[x, 0:1] = zero
        mid[x, NY + 1 : NY + 2] = zero

    @pl.when(flags[0] == 0)
    def _():
        for l in range(2):
            old[l] = sent[l]
            old[2 + l] = kept[l]

    @pl.when(flags[0] != 0)
    def _():
        for l in range(2):
            old[l] = kept[l]
            old[2 + l] = sent[l]

    def substep(ref, y, store, store_reach=None):
        for x in range(LAYERS):
            u = spread_rows(wind[x, pl.ds(y, 8), :])
            west, east = from_west_of(u, spread), from_east_of(u, spread)
            value = within(ref[x, pl.ds(y, 10)], u, held)
            if x > 0:
                value = value + ref[x - 1, pl.ds(y + 1, 8)] * west
            if x < LAYERS - 1:
                value = value + ref[x + 1, pl.ds(y + 1, 8)] * east
            store(x, value)
            if store_reach is not None:
                store_reach(x, west if x < 2 else east)

    def first(b, _):
        y = pl.multiple_of(8 * b, 8)

        def store(x, value):
            mid[x, pl.ds(y + 1, 8)] = value

        def store_reach(x, value):
            reach[x, pl.ds(y, 8)] = value

        substep(old, y, store, store_reach)
        return 0

    def second(b, _):
        y = pl.multiple_of(8 * b, 8)

        def store(x, value):
            field[x, pl.ds(y, 8)] = value

        substep(mid, y, store)
        return 0

    lax.fori_loop(0, NY // 8, first, 0, unroll=True)
    lax.fori_loop(0, NY // 8, second, 0, unroll=True)


def outer_body(
    flags, partner, other, wind, old, inner, reach, constants, field, rounded, halo, change, beyond
):
    odd = flags[0]
    held = tuple(constants[i] for i in range(4))
    spread = held[3]
    zero = jnp.zeros((1, OWN, NZ), F32)
    for side in range(2):
        for ref in (halo, change):
            ref[side, 0:1] = zero
            ref[side, NY + 1 : NY + 2] = zero
    sides = ((partner, 1 - odd), (other, odd))

    def bring(p, _):
        for message, side in sides:
            for r in range(4):
                two = message[(1 - side) * HALF + 4 * p + r].astype(F32).reshape(2, OWN, NZ)
                halo[side, pl.ds(8 * p + 2 * r + 1, 2)] = two
        return 0

    lax.fori_loop(0, NY // 8, bring, 0, unroll=True)

    def through(b, _):
        y = pl.multiple_of(8 * b, 8)
        for message, side in sides:
            edge = 3 * side
            sign = 1.0 - 2.0 * side.astype(F32)
            inside = flags[1 + side].astype(F32)
            far = [
                message[side * HALF + 4 * b + h].astype(F32).reshape(2, OWN, NZ) for h in range(4)
            ]
            far = jnp.concatenate(far, 0)
            winds = message[2 * HALF + b // 2].astype(F32)
            u = spread_rows(jnp.where(lax.rem(b, 2) == 0, winds[0:8], winds[8:16]))
            outward = sign * u
            ten = halo[side, pl.ds(y, 10)]
            value = (
                within(ten, u, held)
                + far * (spread + jnp.maximum(outward, 0.0))
                + old[edge, pl.ds(y + 1, 8)] * (spread - jnp.minimum(outward, 0.0))
            )
            beyond[side, pl.ds(y, 8)] = value * inside
            change[side, pl.ds(y + 1, 8)] = ten[1:9] * reach[edge, pl.ds(y, 8)]
        return 0

    lax.fori_loop(0, NY // 8, through, 0, unroll=True)

    def finish(b, _):
        y = pl.multiple_of(8 * b, 8)
        for x in range(LAYERS):
            side = x // 2
            r = reach[x, pl.ds(y, 8)]
            value = inner[x, pl.ds(y, 8)]
            if x in (0, LAYERS - 1):
                u = spread_rows(wind[x, pl.ds(y, 8), :])
                ten = change[side, pl.ds(y, 10)]
                value = value + within(ten, u, held) + beyond[side, pl.ds(y, 8)] * r
            else:
                value = value + change[side, pl.ds(y + 1, 8)] * r
            field[x, pl.ds(y, 8)] = value
            for h in range(4):
                two = value[2 * h : 2 * h + 2].reshape(16, NZ)
                at = 4 * b + h
                rounded[2 * x + at // PAIRS, lax.rem(at, PAIRS)] = two.astype(BF)
        return 0

    lax.fori_loop(0, NY // 8, finish, 0, unroll=True)


WIDE = 4


def kinetics_body(cells, linear, pairs, out, wide, products):
    def step(q, _):
        parts = []
        for u in range(WIDE):
            x = cells[:, WIDE * q + u].astype(F32)
            parts += [x[:, 0:8, :].reshape(S, NZ), x[:, 8:16, :].reshape(S, NZ)]
        n = jnp.concatenate(parts, 1)
        wide[...] = n
        base = 0
        for g in range(8):
            count = S - 8 * g
            high = n[8 * g :]
            for i in range(8 * g, 8 * g + 8, 2):
                both = [high * wide[r : r + 1, :] for r in (i, i + 1)]
                products[base : base + 2 * count, :] = jnp.concatenate(both, 0).astype(BF)
                base += 2 * count
        gained = jnp.dot(pairs[...], products[...], preferred_element_type=F32)
        straight = jnp.dot(linear[...], n.astype(BF), preferred_element_type=F32)
        total = straight[0:S] + gained - n * straight[S : 2 * S]
        for u in range(WIDE):
            at = 2 * NZ * u
            a = total[:, at : at + NZ].reshape(8, OWN, NZ)
            b = total[:, at + NZ : at + 2 * NZ].reshape(8, OWN, NZ)
            out[:, WIDE * q + u] = jnp.concatenate([a, b], 1).astype(BF)
        return 0

    lax.fori_loop(0, PAIRS // WIDE, step, 0)


def finish_body(field, tendency, out, held, sems):
    copies = []
    for x in range(LAYERS):
        layer = held.at[x].reshape(OWN * NY, NZ)

        def rows(p, _):
            for half in range(2):
                y = half * HALF + 2 * p
                two = STEP * tendency[2 * x + half, p].astype(F32)
                layer[pl.ds(y, OWN, stride=NY), :] = field[x, y] + two[0:8]
                layer[pl.ds(y + 1, OWN, stride=NY), :] = field[x, y + 1] + two[8:16]
            return 0

        lax.fori_loop(0, PAIRS, rows, 0, unroll=True)
        copies.append(pltpu.make_async_copy(held.at[x], out.at[:, x], sems.at[x]))
        copies[x].start()
    for copy in copies:
        copy.wait()


def per_device(density, wind_speed, settling, diffusion, breakup, coag_kernel, pair_target):
    slabs = lax.axis_size("space")
    me = lax.axis_index("space")
    odd = me % 2
    flags = jnp.stack([odd, (me > 0).astype(jnp.int32), (me < slabs - 1).astype(jnp.int32)])
    smem = pl.BlockSpec(memory_space=pltpu.SMEM)
    vmem = pl.BlockSpec(memory_space=pltpu.VMEM)
    hbm = pl.BlockSpec(memory_space=pltpu.HBM)
    message = jax.ShapeDtypeStruct((2 * HALF + NY // 16, 16, NZ), BF)
    block = jax.ShapeDtypeStruct((8, PAIRS, 16, NZ), BF)
    cells_f32 = jax.ShapeDtypeStruct((LAYERS, NY, OWN, NZ), F32)
    padded = (LAYERS, NY + 2, OWN, NZ)

    def pack(first_layer, edge):
        return call(
            pack_body,
            (message, jax.ShapeDtypeStruct((2, NY + 2, OWN, NZ), F32)),
            scratch=(
                pltpu.VMEM((2, OWN, NY, NZ), F32),
                pltpu.VMEM((NY, NZ), F32),
                pltpu.SemaphoreType.DMA((3,)),
            ),
            in_specs=[smem, hbm, hbm],
        )(jnp.stack([first_layer, edge]), density, wind_speed)

    to_other, sent = pack(2 * odd, 3 * odd)
    other = lax.ppermute(to_other, "space", [(i, ((i + 1) ^ 1) - 1) for i in range(1, slabs - 1)])
    to_partner, kept = pack(2 - 2 * odd, 3 - 3 * odd)
    partner = lax.ppermute(to_partner, "space", [(i, i ^ 1) for i in range(slabs)])
    old, inner, reach, constants, linear, pairs = call(
        inner_body,
        (
            jax.ShapeDtypeStruct(padded, F32),
            cells_f32,
            cells_f32,
            jax.ShapeDtypeStruct((4, OWN, NZ), F32),
            jax.ShapeDtypeStruct((2 * S, S), BF),
            jax.ShapeDtypeStruct((S, PAIR_ROWS), BF),
        ),
        scratch=(pltpu.VMEM(padded, F32), pltpu.VMEM((PAIR_ROWS, NZ), F32)),
        in_specs=[smem] * 3 + [vmem] * 6,
    )(flags, settling, diffusion, sent, kept, wind_speed, coag_kernel, pair_target, breakup)
    field, rounded = call(
        outer_body,
        (cells_f32, block),
        scratch=(
            pltpu.VMEM((2, NY + 2, OWN, NZ), F32),
            pltpu.VMEM((2, NY + 2, OWN, NZ), F32),
            pltpu.VMEM((2, NY, OWN, NZ), F32),
        ),
        in_specs=[smem] + [vmem] * 7,
    )(flags, partner, other, wind_speed, old, inner, reach, constants)
    cells = lax.all_to_all(rounded, "sec", split_axis=0, concat_axis=0, tiled=True)
    width = 2 * NZ * WIDE
    tendency = call(
        kinetics_body,
        block,
        scratch=(pltpu.VMEM((S, width), F32), pltpu.VMEM((PAIR_ROWS, width), BF)),
    )(cells, linear, pairs)
    returned = lax.all_to_all(tendency, "sec", split_axis=0, concat_axis=0, tiled=True)
    return call(
        finish_body,
        jax.ShapeDtypeStruct((OWN, LAYERS, NY, NZ), F32),
        scratch=(pltpu.VMEM((LAYERS, OWN, NY, NZ), F32), pltpu.SemaphoreType.DMA((LAYERS,))),
        in_specs=[vmem, vmem],
        out_specs=hbm,
    )(field, returned)


def solution(mesh):
    in_specs = (
        P("sec", "space", None, None),
        P("space", None, None),
        P("sec"),
        P("sec"),
        P(),
        P(),
        P(),
    )
    out_specs = P("sec", "space", None, None)
    return jax.shard_map(
        per_device, mesh=mesh, in_specs=in_specs, out_specs=out_specs, check_vma=False
    )
```

```python
import functools

import jax
import jax.numpy as jnp
from jax import lax
from jax.experimental import pallas as pl
from jax.experimental.pallas import tpu as pltpu
from jax.sharding import PartitionSpec as P

BF = jnp.bfloat16
F32 = jnp.float32
S = 64
OWN = 8
LAYERS = 4
NY = 64
NZ = 128
HALF = 32
PAIRS = HALF // 2
STEP = 0.25
BLOCKS = 36
DEPTH = BLOCKS * S + 2 * S
LIMIT = 48 * 1024 * 1024


def call(body, out_shape, scratch=(), **specs):
    return pl.pallas_call(
        body,
        out_shape=out_shape,
        scratch_shapes=scratch,
        compiler_params=pltpu.CompilerParams(vmem_limit_bytes=LIMIT),
        **specs,
    )


def oddness():
    return lax.rem(lax.axis_index("space"), 2)


def bring_layer(loaded, out, x):
    zero = jnp.zeros((1, OWN, NZ), F32)
    out[x, 0:1] = zero
    out[x, NY + 1 : NY + 2] = zero

    def rows(p, _):
        for r in range(8):
            out[x, 8 * p + r + 1] = loaded[pl.ds(8 * p + r, OWN, stride=NY), :]
        return 0

    lax.fori_loop(0, NY // 8, rows, 0, unroll=True)


def pack_layer(layer, x, out, at):
    def rows(p, _):
        for r in range(4):
            two = layer[x, pl.ds(8 * p + 2 * r + 1, 2)].reshape(16, NZ)
            out[at + 4 * p + r] = two.astype(BF)
        return 0

    lax.fori_loop(0, NY // 8, rows, 0, unroll=True)


def pack_body(density, wind, out, old, loaded, sems):
    base = 2 - 2 * oddness()
    copies = [
        pltpu.make_async_copy(density.at[:, base + l], loaded.at[l], sems.at[l]) for l in range(2)
    ]
    for copy in copies:
        copy.start()
    for t in range(NY // 16):
        out[2 * HALF + t] = wind[0, 16 * t : 16 * t + 16, :]
    for l in range(2):
        copies[l].wait()
        bring_layer(loaded.at[l].reshape(OWN * NY, NZ), old, l)
        pack_layer(old, l, out, l * HALF)


def block_pairs():
    for g in range(5):
        for q in range(4 if g == 4 else 8):
            yield g, 8 * g + q, (36 + q if g == 4 else (64 - 8 * g + q) % S)


def table_body(kernel, target, breakup, table, rows):
    lane = lax.broadcasted_iota(jnp.int32, (S, NZ), 1)
    second = lane >= S
    column = jnp.where(second, lane - S, lane)

    def blocks(a):
        parts = [a[0:8]]
        for g in range(1, 5):
            count = 4 if g == 4 else 8
            other = 36 if g == 4 else 8 * (8 - g)
            moved = pltpu.roll(a, S + 8 * g, 1)[other : other + count]
            own = a[8 * g : 8 * g + count]
            parts.append(jnp.where(column[0:count] >= 8 * g, own, moved))
        return parts

    def store(at, a):
        for g, part in enumerate(blocks(a)):
            rows[at, 8 * g : 8 * g + part.shape[0], :] = part

    def twice(a):
        return jnp.concatenate([a, a], 1)

    rates = kernel[...].astype(BF).astype(F32)
    targets = target[...].astype(F32)
    j = blocks(column.astype(F32))
    i = blocks(lax.broadcasted_iota(jnp.int32, (S, NZ), 0).astype(F32))
    store(0, twice(targets))
    store(1, twice(jnp.transpose(targets)))
    for g, (one, two) in enumerate(zip(blocks(twice(rates)), blocks(twice(jnp.transpose(rates))))):
        rows[2, 8 * g : 8 * g + one.shape[0], :] = jnp.where(j[g] >= i[g], one, 0.0)
        rows[3, 8 * g : 8 * g + one.shape[0], :] = jnp.where(j[g] > i[g], two, 0.0)
    k = lax.broadcasted_iota(jnp.int32, (S, NZ), 0).astype(F32)
    for t in range(BLOCKS // 2):
        to, to_t, rate, rate_t = [
            jnp.where(second[0:1], rows[q, 2 * t + 1 : 2 * t + 2, :], rows[q, 2 * t : 2 * t + 1, :])
            for q in range(4)
        ]
        one = jnp.where(to == k, rate, 0.0) + jnp.where(to_t == k, rate_t, 0.0)
        table[0:S, t * NZ : (t + 1) * NZ] = one.astype(BF)
    table[S:, : BLOCKS * S] = jnp.zeros((S, BLOCKS * S), BF)
    none = jnp.zeros((S, S), F32)
    table[0:S, BLOCKS * S :] = jnp.concatenate([breakup[...].astype(F32), none], 1).astype(BF)
    table[S:, BLOCKS * S :] = jnp.concatenate([rates, none], 1).astype(BF)


def spread_rows(rows):
    return jnp.broadcast_to(rows[:, None, :], (8, OWN, NZ))


def within(ten, u, constants):
    here, from_above, from_below, spread = constants
    c = ten[1:9]
    return (
        c * (here - jnp.abs(u))
        + pltpu.roll(c, NZ - 1, 2) * from_above
        + pltpu.roll(c, 1, 2) * from_below
        + (ten[0:8] + ten[2:10]) * spread
    )


def from_west_of(u, spread):
    return spread + jnp.maximum(u, 0.0)


def from_east_of(u, spread):
    return spread - jnp.minimum(u, 0.0)


def per_section(ref):
    row = lax.broadcasted_iota(jnp.int32, (OWN, OWN), 0)
    column = lax.broadcasted_iota(jnp.int32, (OWN, OWN), 1)
    spread = jnp.where(row == column, jnp.broadcast_to(ref[...], (OWN, OWN)), 0.0)
    return jnp.broadcast_to(jnp.sum(spread, axis=1, keepdims=True), (OWN, NZ))


def inner_body(
    settling, diffusion, density, kept, wind, kernel, target, breakup,
    old, field, reach, constants, table, mid, rows,
):
    table_body(kernel, target, breakup, table, rows)
    sink, spread = per_section(settling), per_section(diffusion)
    lane = lax.broadcasted_iota(jnp.int32, (OWN, NZ), 1)
    held = (
        1.0 - sink - 6.0 * spread,
        jnp.where(lane == NZ - 1, 0.0, sink + spread),
        jnp.where(lane == 0, 0.0, spread),
        spread,
    )
    for i in range(4):
        constants[i] = held[i]
    zero = jnp.zeros((1, OWN, NZ), F32)
    for x in range(LAYERS):
        mid[x, 0:1] = zero
        mid[x, NY + 1 : NY + 2] = zero

    rest = 2 * oddness()
    own = 2 - rest
    for l in range(2):
        old[own + l] = kept[l]
        for y in (0, NY + 1):
            old[rest + l, y : y + 1] = zero
        start = (rest + l) * NY
        for y in range(NY):
            old[rest + l, y + 1] = density[pl.ds(start + y, OWN, stride=LAYERS * NY), :]

    def substep(ref, y, store, store_reach=None):
        for x in range(LAYERS):
            u = spread_rows(wind[x, pl.ds(y, 8), :])
            west, east = from_west_of(u, spread), from_east_of(u, spread)
            value = within(ref[x, pl.ds(y, 10)], u, held)
            if x > 0:
                value = value + ref[x - 1, pl.ds(y + 1, 8)] * west
            if x < LAYERS - 1:
                value = value + ref[x + 1, pl.ds(y + 1, 8)] * east
            store(x, value)
            if store_reach is not None:
                store_reach(x, west if x < 2 else east)

    def first(b, _):
        y = pl.multiple_of(8 * b, 8)

        def store(x, value):
            mid[x, pl.ds(y + 1, 8)] = value

        def store_reach(x, value):
            reach[x, pl.ds(y, 8)] = value

        substep(old, y, store, store_reach)
        return 0

    def second(b, _):
        y = pl.multiple_of(8 * b, 8)

        def store(x, value):
            field[x, pl.ds(y, 8)] = value

        substep(mid, y, store)
        return 0

    lax.fori_loop(0, NY // 8, first, 0, unroll=True)
    lax.fori_loop(0, NY // 8, second, 0, unroll=True)


def side_body(
    plain, slabs, message, wind, old, inner, reach, constants, *refs
):
    if plain:
        done, field, rounded, halo, change, beyond, raw = refs
    else:
        field, rounded, halo, change, beyond = refs
    odd = oddness()
    side = odd if plain else 1 - odd
    edge = 3 * side
    next_layer = 1 + side
    sign = 1.0 - 2.0 * side.astype(F32)
    inside = (lax.axis_index("space") != side * (slabs - 1)).astype(F32)
    held = tuple(constants[i] for i in range(4))
    spread = held[3]
    zero = jnp.zeros((1, OWN, NZ), F32)
    for ref in (halo, change):
        ref[0:1] = zero
        ref[NY + 1 : NY + 2] = zero
    if plain:
        for t in range(LAYERS):
            rounded[t] = done[t]
        for s in range(OWN):
            for l in range(2):
                raw[l, s * NY : (s + 1) * NY, :] = message[2 * s + l].astype(F32)
        for y in range(NY):
            halo[y + 1] = raw[1 - side, pl.ds(y, OWN, stride=NY), :]
    else:
        for p in range(HALF):
            two = message[(1 - side) * HALF + p].astype(F32).reshape(2, OWN, NZ)
            halo[2 * p + 1 : 2 * p + 3] = two

    for b in range(NY // 8):
        y = 8 * b
        if plain:
            far = [raw[side, pl.ds(y + r, OWN, stride=NY), :][None] for r in range(8)]
            winds = message[2 * OWN + 1 - side, 16 * (b // 2) : 16 * (b // 2) + 16, :].astype(F32)
        else:
            far = [
                message[side * HALF + 4 * b + h].astype(F32).reshape(2, OWN, NZ) for h in range(4)
            ]
            winds = message[2 * HALF + b // 2].astype(F32)
        far = jnp.concatenate(far, 0)
        u = spread_rows(winds[8 * (b % 2) : 8 * (b % 2) + 8])
        outward = sign * u
        ten = halo[y : y + 10]
        value = (
            within(ten, u, held)
            + far * (spread + jnp.maximum(outward, 0.0))
            + old[edge, y + 1 : y + 9] * (spread - jnp.minimum(outward, 0.0))
        )
        beyond[y : y + 8] = value * inside
        change[y + 1 : y + 9] = ten[1:9] * reach[edge, y : y + 8]

    for b in range(NY // 8):
        y = 8 * b
        u = spread_rows(wind[edge, y : y + 8, :])
        ten = change[y : y + 10]
        outer = inner[edge, y : y + 8] + within(ten, u, held)
        outer = outer + beyond[y : y + 8] * reach[edge, y : y + 8]
        second = inner[next_layer, y : y + 8] + ten[1:9] * reach[next_layer, y : y + 8]
        for at, value in ((side, outer), (1 - side, second)):
            field[at, y : y + 8] = value
            for h in range(4):
                two = value[2 * h : 2 * h + 2].reshape(16, NZ)
                p = 4 * b + h
                slot = (LAYERS if plain else 0) + 2 * at + p // PAIRS
                rounded[slot, p % PAIRS] = two.astype(BF)


WIDE = 16


def kinetics_body(cells, table, out, wide, products):
    products[DEPTH - S :, :] = jnp.zeros((S, 2 * NZ * WIDE), BF)

    def step(q, _):
        parts = []
        for u in range(WIDE):
            x = cells[:, WIDE * q + u].astype(F32)
            parts += [x[:, 0:8, :].reshape(S, NZ), x[:, 8:16, :].reshape(S, NZ)]
        n = jnp.concatenate(parts, 1)
        wide[...] = n
        for b, (g, i, other) in enumerate(block_pairs()):
            n_i, n_other = wide[i : i + 1, :], wide[other : other + 1, :]
            rows = []
            for t in range(8):
                if t < g:
                    at = 8 * (t + 8 - g)
                    rows.append(n[at : at + 8] * n_other)
                else:
                    rows.append(n[8 * t : 8 * t + 8] * n_i)
            products[S * b : S * (b + 1), :] = jnp.concatenate(rows, 0).astype(BF)
        products[BLOCKS * S : BLOCKS * S + S, :] = n.astype(BF)
        sums = jnp.dot(table[...], products[...], preferred_element_type=F32)
        total = sums[0:S] - n * sums[S:]
        for u in range(WIDE):
            at = 2 * NZ * u
            a = total[:, at : at + NZ].reshape(8, OWN, NZ)
            b = total[:, at + NZ : at + 2 * NZ].reshape(8, OWN, NZ)
            out[:, WIDE * q + u] = jnp.concatenate([a, b], 1).astype(BF)
        return 0

    lax.fori_loop(0, PAIRS // WIDE, step, 0)


def finish_body(near, far, tendency, out, held, sems):
    odd = oddness()
    copies = []
    for x in range(LAYERS):
        layer = held.at[x].reshape(OWN * NY, NZ)
        field, at = (near, x) if x < 2 else (far, x - 2)

        def rows(p, _):
            for half in range(2):
                y = half * HALF + 2 * p
                two = STEP * tendency[2 * x + half, p].astype(F32)
                layer[pl.ds(y, OWN, stride=NY), :] = field[at, y] + two[0:8]
                layer[pl.ds(y + 1, OWN, stride=NY), :] = field[at, y + 1] + two[8:16]
            return 0

        lax.fori_loop(0, PAIRS, rows, 0, unroll=True)
        place = at + 2 * (1 - odd) if x < 2 else at + 2 * odd
        copies.append(pltpu.make_async_copy(held.at[x], out.at[:, place], sems.at[x]))
        copies[x].start()
    for copy in copies:
        copy.wait()


def per_device(density, wind_speed, settling, diffusion, breakup, coag_kernel, pair_target):
    slabs = lax.axis_size("space")
    odd = oddness()
    vmem = pl.BlockSpec(memory_space=pltpu.VMEM)
    hbm = pl.BlockSpec(memory_space=pltpu.HBM)
    message = jax.ShapeDtypeStruct((2 * HALF + NY // 16, 16, NZ), BF)
    block = jax.ShapeDtypeStruct((8, PAIRS, 16, NZ), BF)
    cells_f32 = jax.ShapeDtypeStruct((LAYERS, NY, OWN, NZ), F32)
    padded = (LAYERS, NY + 2, OWN, NZ)

    both = jnp.concatenate([density, wind_speed[None]], 0)
    to_other = lax.dynamic_slice_in_dim(both, 2 * odd, 2, 1).astype(BF).reshape(2 * OWN + 2, NY, NZ)
    other = lax.ppermute(to_other, "space", [(i, ((i + 1) ^ 1) - 1) for i in range(1, slabs - 1)])
    wind_held = lax.optimization_barrier(wind_speed)
    to_partner, kept = call(
        pack_body,
        (message, jax.ShapeDtypeStruct((2, NY + 2, OWN, NZ), F32)),
        scratch=(
            pltpu.VMEM((2, OWN, NY, NZ), F32),
            pltpu.SemaphoreType.DMA((2,)),
        ),
        in_specs=[hbm, vmem],
    )(density, jnp.where(odd == 0, wind_held[LAYERS - 1 :], wind_held[0:1]).astype(BF))
    partner = lax.ppermute(to_partner, "space", [(i, i ^ 1) for i in range(slabs)])
    old, inner, reach, constants, table = call(
        inner_body,
        (
            jax.ShapeDtypeStruct(padded, F32),
            cells_f32,
            cells_f32,
            jax.ShapeDtypeStruct((4, OWN, NZ), F32),
            jax.ShapeDtypeStruct((2 * S, DEPTH), BF),
        ),
        scratch=(pltpu.VMEM(padded, F32), pltpu.VMEM((4, BLOCKS, NZ), F32)),
    )(
        settling.reshape(1, OWN), diffusion.reshape(1, OWN), density.reshape(OWN * LAYERS * NY, NZ), kept, wind_speed,
        coag_kernel, pair_target, breakup,
    )
    half = jax.ShapeDtypeStruct((2, NY, OWN, NZ), F32)
    half_block = jax.ShapeDtypeStruct((4, PAIRS, 16, NZ), BF)
    row_block = (NY + 2, OWN, NZ)
    scratch = (pltpu.VMEM(row_block, F32), pltpu.VMEM(row_block, F32), pltpu.VMEM((NY, OWN, NZ), F32))
    rest = (wind_speed, old, inner, reach, constants)
    near, near_rounded = call(
        functools.partial(side_body, False, slabs),
        (half, half_block),
        scratch=scratch,
    )(partner, *rest)
    far, rounded = call(
        functools.partial(side_body, True, slabs),
        (half, block),
        scratch=scratch + (pltpu.VMEM((2, OWN * NY, NZ), F32),),
    )(other, *rest, near_rounded)
    cells = lax.all_to_all(rounded, "sec", split_axis=0, concat_axis=0, tiled=True)
    width = 2 * NZ * WIDE
    tendency = call(
        kinetics_body,
        block,
        scratch=(pltpu.VMEM((S, width), F32), pltpu.VMEM((DEPTH, width), BF)),
    )(cells, table)
    returned = lax.all_to_all(tendency, "sec", split_axis=0, concat_axis=0, tiled=True)
    return call(
        finish_body,
        jax.ShapeDtypeStruct((OWN, LAYERS, NY, NZ), F32),
        scratch=(pltpu.VMEM((LAYERS, OWN, NY, NZ), F32), pltpu.SemaphoreType.DMA((LAYERS,))),
        in_specs=[vmem, vmem, vmem],
        out_specs=hbm,
    )(near, far, returned)


def solution(mesh):
    in_specs = (
        P("sec", "space", None, None),
        P("space", None, None),
        P("sec"),
        P("sec"),
        P(),
        P(),
        P(),
    )
    out_specs = P("sec", "space", None, None)
    return jax.shard_map(
        per_device, mesh=mesh, in_specs=in_specs, out_specs=out_specs, check_vma=False
    )
```

```python
import functools

import jax
import jax.numpy as jnp
from jax import lax
from jax.experimental import pallas as pl
from jax.experimental.pallas import tpu as pltpu
from jax.sharding import PartitionSpec as P

BF = jnp.bfloat16
F32 = jnp.float32
S = 64
OWN = 8
LAYERS = 4
NY = 64
NZ = 128
HALF = 32
PAIRS = HALF // 2
STEP = 0.25
BLOCKS = 36
DEPTH = BLOCKS * S + 2 * S
LIMIT = 48 * 1024 * 1024


def call(body, out_shape, scratch=(), **specs):
    return pl.pallas_call(
        body,
        out_shape=out_shape,
        scratch_shapes=scratch,
        compiler_params=pltpu.CompilerParams(vmem_limit_bytes=LIMIT),
        **specs,
    )


def oddness():
    return lax.rem(lax.axis_index("space"), 2)


def swapped(block):
    return jnp.swapaxes(block, 0, 1)


def bring_layer(loaded, out, x):
    zero = jnp.zeros((1, OWN, NZ), F32)
    out[x, 0:1] = zero
    out[x, NY + 1 : NY + 2] = zero
    for y in range(0, NY, 8):
        out[x, y + 1 : y + 9] = swapped(loaded[:, y : y + 8, :])


def pack_layer(layer, x, out, at):
    def rows(p, _):
        for r in range(4):
            two = layer[x, pl.ds(8 * p + 2 * r + 1, 2)].reshape(16, NZ)
            out[at + 4 * p + r] = two.astype(BF)
        return 0

    lax.fori_loop(0, NY // 8, rows, 0, unroll=True)


def pack_body(density, wind, out, old, loaded, sems):
    base = 2 - 2 * oddness()
    copies = [
        pltpu.make_async_copy(density.at[:, base + l], loaded.at[l], sems.at[l]) for l in range(2)
    ]
    for copy in copies:
        copy.start()
    for t in range(NY // 16):
        out[2 * HALF + t] = wind[0, 16 * t : 16 * t + 16, :]
    for l in range(2):
        copies[l].wait()
        bring_layer(loaded.at[l], old, l)
        pack_layer(old, l, out, l * HALF)


def block_pairs():
    for g in range(5):
        for q in range(4 if g == 4 else 8):
            yield g, 8 * g + q, (36 + q if g == 4 else (64 - 8 * g + q) % S)


def table_body(kernel, target, breakup, table, rows):
    lane = lax.broadcasted_iota(jnp.int32, (S, NZ), 1)
    second = lane >= S
    column = jnp.where(second, lane - S, lane)

    def blocks(a):
        parts = [a[0:8]]
        for g in range(1, 5):
            count = 4 if g == 4 else 8
            other = 36 if g == 4 else 8 * (8 - g)
            moved = pltpu.roll(a, S + 8 * g, 1)[other : other + count]
            own = a[8 * g : 8 * g + count]
            parts.append(jnp.where(column[0:count] >= 8 * g, own, moved))
        return parts

    def store(at, a):
        for g, part in enumerate(blocks(a)):
            rows[at, 8 * g : 8 * g + part.shape[0], :] = part

    def twice(a):
        return jnp.concatenate([a, a], 1)

    rates = kernel[...].astype(BF).astype(F32)
    targets = target[...].astype(F32)
    j = blocks(column.astype(F32))
    i = blocks(lax.broadcasted_iota(jnp.int32, (S, NZ), 0).astype(F32))
    store(0, twice(targets))
    store(1, twice(jnp.transpose(targets)))
    for g, (one, two) in enumerate(zip(blocks(twice(rates)), blocks(twice(jnp.transpose(rates))))):
        rows[2, 8 * g : 8 * g + one.shape[0], :] = jnp.where(j[g] >= i[g], one, 0.0)
        rows[3, 8 * g : 8 * g + one.shape[0], :] = jnp.where(j[g] > i[g], two, 0.0)
    k = lax.broadcasted_iota(jnp.int32, (S, NZ), 0).astype(F32)
    for t in range(BLOCKS // 2):
        to, to_t, rate, rate_t = [
            jnp.where(second[0:1], rows[q, 2 * t + 1 : 2 * t + 2, :], rows[q, 2 * t : 2 * t + 1, :])
            for q in range(4)
        ]
        one = jnp.where(to == k, rate, 0.0) + jnp.where(to_t == k, rate_t, 0.0)
        table[0:S, t * NZ : (t + 1) * NZ] = one.astype(BF)
    table[S:, : BLOCKS * S] = jnp.zeros((S, BLOCKS * S), BF)
    none = jnp.zeros((S, S), F32)
    table[0:S, BLOCKS * S :] = jnp.concatenate([breakup[...].astype(F32), none], 1).astype(BF)
    table[S:, BLOCKS * S :] = jnp.concatenate([rates, none], 1).astype(BF)


def spread_rows(rows):
    return jnp.broadcast_to(rows[:, None, :], (8, OWN, NZ))


def within(ten, u, constants):
    here, from_above, from_below, spread = constants
    c = ten[1:9]
    return (
        c * (here - jnp.abs(u))
        + pltpu.roll(c, NZ - 1, 2) * from_above
        + pltpu.roll(c, 1, 2) * from_below
        + (ten[0:8] + ten[2:10]) * spread
    )


def from_west_of(u, spread):
    return spread + jnp.maximum(u, 0.0)


def from_east_of(u, spread):
    return spread - jnp.minimum(u, 0.0)


def per_section(ref):
    row = lax.broadcasted_iota(jnp.int32, (OWN, OWN), 0)
    column = lax.broadcasted_iota(jnp.int32, (OWN, OWN), 1)
    spread = jnp.where(row == column, jnp.broadcast_to(ref[...], (OWN, OWN)), 0.0)
    return jnp.broadcast_to(jnp.sum(spread, axis=1, keepdims=True), (OWN, NZ))


def inner_body(
    settling, diffusion, density, kept, wind, kernel, target, breakup,
    old, field, reach, constants, table, mid, rows,
):
    table_body(kernel, target, breakup, table, rows)
    sink, spread = per_section(settling), per_section(diffusion)
    lane = lax.broadcasted_iota(jnp.int32, (OWN, NZ), 1)
    held = (
        1.0 - sink - 6.0 * spread,
        jnp.where(lane == NZ - 1, 0.0, sink + spread),
        jnp.where(lane == 0, 0.0, spread),
        spread,
    )
    for i in range(4):
        constants[i] = held[i]
    zero = jnp.zeros((1, OWN, NZ), F32)
    for x in range(LAYERS):
        mid[x, 0:1] = zero
        mid[x, NY + 1 : NY + 2] = zero

    rest = 2 * oddness()
    own = 2 - rest
    for l in range(2):
        old[own + l] = kept[l]
        bring_layer(density.at[:, rest + l], old, rest + l)

    def substep(ref, y, store, store_reach=None):
        for x in range(LAYERS):
            u = spread_rows(wind[x, pl.ds(y, 8), :])
            west, east = from_west_of(u, spread), from_east_of(u, spread)
            value = within(ref[x, pl.ds(y, 10)], u, held)
            if x > 0:
                value = value + ref[x - 1, pl.ds(y + 1, 8)] * west
            if x < LAYERS - 1:
                value = value + ref[x + 1, pl.ds(y + 1, 8)] * east
            store(x, value)
            if store_reach is not None:
                store_reach(x, west if x < 2 else east)

    def first(b, _):
        y = pl.multiple_of(8 * b, 8)

        def store(x, value):
            mid[x, pl.ds(y + 1, 8)] = value

        def store_reach(x, value):
            reach[x, pl.ds(y, 8)] = value

        substep(old, y, store, store_reach)
        return 0

    def second(b, _):
        y = pl.multiple_of(8 * b, 8)

        def store(x, value):
            field[x, pl.ds(y, 8)] = value

        substep(mid, y, store)
        return 0

    lax.fori_loop(0, NY // 8, first, 0, unroll=True)
    lax.fori_loop(0, NY // 8, second, 0, unroll=True)


def side_body(
    plain, slabs, message, wind, old, inner, reach, constants, *refs
):
    if plain:
        done, field, rounded, halo, change, beyond, far = refs
    else:
        field, rounded, halo, change, beyond = refs
    odd = oddness()
    side = odd if plain else 1 - odd
    edge = 3 * side
    next_layer = 1 + side
    sign = 1.0 - 2.0 * side.astype(F32)
    inside = (lax.axis_index("space") != side * (slabs - 1)).astype(F32)
    held = tuple(constants[i] for i in range(4))
    spread = held[3]
    zero = jnp.zeros((1, OWN, NZ), F32)
    for ref in (halo, change):
        ref[0:1] = zero
        ref[NY + 1 : NY + 2] = zero
    if plain:
        for t in range(LAYERS):
            rounded[t] = done[t]
        for y in range(0, NY, 16):
            for l, out, first in ((1 - side, halo, 1), (side, far, 0)):
                rows = [message[2 * s + l, y : y + 16, :].astype(F32)[None] for s in range(OWN)]
                rows = jnp.concatenate(rows, 0)
                out[y + first : y + first + 8] = swapped(rows[:, 0:8])
                out[y + first + 8 : y + first + 16] = swapped(rows[:, 8:16])
    else:
        for p in range(HALF):
            two = message[(1 - side) * HALF + p].astype(F32).reshape(2, OWN, NZ)
            halo[2 * p + 1 : 2 * p + 3] = two

    for b in range(NY // 8):
        y = 8 * b
        if plain:
            farther = far[y : y + 8]
            winds = message[2 * OWN + 1 - side, 16 * (b // 2) : 16 * (b // 2) + 16, :].astype(F32)
        else:
            farther = [
                message[side * HALF + 4 * b + h].astype(F32).reshape(2, OWN, NZ) for h in range(4)
            ]
            farther = jnp.concatenate(farther, 0)
            winds = message[2 * HALF + b // 2].astype(F32)
        u = spread_rows(winds[8 * (b % 2) : 8 * (b % 2) + 8])
        outward = sign * u
        ten = halo[y : y + 10]
        value = (
            within(ten, u, held)
            + farther * (spread + jnp.maximum(outward, 0.0))
            + old[edge, y + 1 : y + 9] * (spread - jnp.minimum(outward, 0.0))
        )
        beyond[y : y + 8] = value * inside
        change[y + 1 : y + 9] = ten[1:9] * reach[edge, y : y + 8]

    for b in range(NY // 8):
        y = 8 * b
        u = spread_rows(wind[edge, y : y + 8, :])
        ten = change[y : y + 10]
        outer = inner[edge, y : y + 8] + within(ten, u, held)
        outer = outer + beyond[y : y + 8] * reach[edge, y : y + 8]
        second = inner[next_layer, y : y + 8] + ten[1:9] * reach[next_layer, y : y + 8]
        for at, value in ((side, outer), (1 - side, second)):
            field[at, y : y + 8] = value
            for h in range(4):
                two = value[2 * h : 2 * h + 2].reshape(16, NZ)
                p = 4 * b + h
                slot = (LAYERS if plain else 0) + 2 * at + p // PAIRS
                rounded[slot, p % PAIRS] = two.astype(BF)


WIDE = 16


def kinetics_body(cells, table, out, wide, products):
    products[DEPTH - S :, :] = jnp.zeros((S, 2 * NZ * WIDE), BF)

    def step(q, _):
        parts = []
        for u in range(WIDE):
            x = cells[:, WIDE * q + u].astype(F32)
            parts += [x[:, 0:8, :].reshape(S, NZ), x[:, 8:16, :].reshape(S, NZ)]
        n = jnp.concatenate(parts, 1)
        wide[...] = n
        for b, (g, i, other) in enumerate(block_pairs()):
            n_i, n_other = wide[i : i + 1, :], wide[other : other + 1, :]
            rows = []
            for t in range(8):
                if t < g:
                    at = 8 * (t + 8 - g)
                    rows.append(n[at : at + 8] * n_other)
                else:
                    rows.append(n[8 * t : 8 * t + 8] * n_i)
            products[S * b : S * (b + 1), :] = jnp.concatenate(rows, 0).astype(BF)
        products[BLOCKS * S : BLOCKS * S + S, :] = n.astype(BF)
        sums = jnp.dot(table[...], products[...], preferred_element_type=F32)
        total = sums[0:S] - n * sums[S:]
        for u in range(WIDE):
            at = 2 * NZ * u
            a = total[:, at : at + NZ].reshape(8, OWN, NZ)
            b = total[:, at + NZ : at + 2 * NZ].reshape(8, OWN, NZ)
            out[:, WIDE * q + u] = jnp.concatenate([a, b], 1).astype(BF)
        return 0

    lax.fori_loop(0, PAIRS // WIDE, step, 0)


def finish_body(near, far, tendency, out, held, sems):
    odd = oddness()
    copies = []
    for slot in range(2 * LAYERS):
        x, first = slot // 2, slot % 2 * HALF
        field, at = (near, x) if x < 2 else (far, x - 2)
        place = at + 2 * (1 - odd) if x < 2 else at + 2 * odd
        for y in range(0, HALF, 8):
            change = [tendency[slot, y // 2 + r].astype(F32).reshape(2, OWN, NZ) for r in range(4)]
            value = field[at, first + y : first + y + 8] + STEP * jnp.concatenate(change, 0)
            held[slot, :, y : y + 8, :] = swapped(value)
        target = out.at[:, place, pl.ds(first, HALF)]
        copies.append(pltpu.make_async_copy(held.at[slot], target, sems.at[slot]))
        copies[slot].start()
    for copy in copies:
        copy.wait()


def per_device(density, wind_speed, settling, diffusion, breakup, coag_kernel, pair_target):
    slabs = lax.axis_size("space")
    odd = oddness()
    vmem = pl.BlockSpec(memory_space=pltpu.VMEM)
    hbm = pl.BlockSpec(memory_space=pltpu.HBM)
    message = jax.ShapeDtypeStruct((2 * HALF + NY // 16, 16, NZ), BF)
    block = jax.ShapeDtypeStruct((8, PAIRS, 16, NZ), BF)
    cells_f32 = jax.ShapeDtypeStruct((LAYERS, NY, OWN, NZ), F32)
    padded = (LAYERS, NY + 2, OWN, NZ)

    both = jnp.concatenate([density, wind_speed[None]], 0)
    to_other = lax.dynamic_slice_in_dim(both, 2 * odd, 2, 1).astype(BF).reshape(2 * OWN + 2, NY, NZ)
    other = lax.ppermute(to_other, "space", [(i, ((i + 1) ^ 1) - 1) for i in range(1, slabs - 1)])
    wind_held = lax.optimization_barrier(wind_speed)
    to_partner, kept = call(
        pack_body,
        (message, jax.ShapeDtypeStruct((2, NY + 2, OWN, NZ), F32)),
        scratch=(
            pltpu.VMEM((2, OWN, NY, NZ), F32),
            pltpu.SemaphoreType.DMA((2,)),
        ),
        in_specs=[hbm, vmem],
    )(density, jnp.where(odd == 0, wind_held[LAYERS - 1 :], wind_held[0:1]).astype(BF))
    partner = lax.ppermute(to_partner, "space", [(i, i ^ 1) for i in range(slabs)])
    old, inner, reach, constants, table = call(
        inner_body,
        (
            jax.ShapeDtypeStruct(padded, F32),
            cells_f32,
            cells_f32,
            jax.ShapeDtypeStruct((4, OWN, NZ), F32),
            jax.ShapeDtypeStruct((2 * S, DEPTH), BF),
        ),
        scratch=(pltpu.VMEM(padded, F32), pltpu.VMEM((4, BLOCKS, NZ), F32)),
    )(
        settling.reshape(1, OWN), diffusion.reshape(1, OWN), density, kept, wind_speed,
        coag_kernel, pair_target, breakup,
    )
    half = jax.ShapeDtypeStruct((2, NY, OWN, NZ), F32)
    half_block = jax.ShapeDtypeStruct((4, PAIRS, 16, NZ), BF)
    row_block = (NY + 2, OWN, NZ)
    scratch = (pltpu.VMEM(row_block, F32), pltpu.VMEM(row_block, F32), pltpu.VMEM((NY, OWN, NZ), F32))
    rest = (wind_speed, old, inner, reach, constants)
    near, near_rounded = call(
        functools.partial(side_body, False, slabs),
        (half, half_block),
        scratch=scratch,
    )(partner, *rest)
    far, rounded = call(
        functools.partial(side_body, True, slabs),
        (half, block),
        scratch=scratch + (pltpu.VMEM((NY, OWN, NZ), F32),),
    )(other, *rest, near_rounded)
    cells = lax.all_to_all(rounded, "sec", split_axis=0, concat_axis=0, tiled=True)
    width = 2 * NZ * WIDE
    tendency = call(
        kinetics_body,
        block,
        scratch=(pltpu.VMEM((S, width), F32), pltpu.VMEM((DEPTH, width), BF)),
    )(cells, table)
    returned = lax.all_to_all(tendency, "sec", split_axis=0, concat_axis=0, tiled=True)
    return call(
        finish_body,
        jax.ShapeDtypeStruct((OWN, LAYERS, NY, NZ), F32),
        scratch=(
            pltpu.VMEM((2 * LAYERS, OWN, HALF, NZ), F32),
            pltpu.SemaphoreType.DMA((2 * LAYERS,)),
        ),
        in_specs=[vmem, vmem, vmem],
        out_specs=hbm,
    )(near, far, returned)


def solution(mesh):
    in_specs = (
        P("sec", "space", None, None),
        P("space", None, None),
        P("sec"),
        P("sec"),
        P(),
        P(),
        P(),
    )
    out_specs = P("sec", "space", None, None)
    return jax.shard_map(
        per_device, mesh=mesh, in_specs=in_specs, out_specs=out_specs, check_vma=False
    )
```

```python
import functools

import jax
import jax.numpy as jnp
from jax import lax
from jax.experimental import pallas as pl
from jax.experimental.pallas import tpu as pltpu
from jax.sharding import PartitionSpec as P

BF = jnp.bfloat16
F32 = jnp.float32
S = 64
OWN = 8
LAYERS = 4
NY = 64
NZ = 128
HALF = 32
PAIRS = HALF // 2
STEP = 0.25
BLOCKS = 36
DEPTH = BLOCKS * S + S
LIMIT = 48 * 1024 * 1024


def call(body, out_shape, scratch=(), **specs):
    return pl.pallas_call(
        body,
        out_shape=out_shape,
        scratch_shapes=scratch,
        compiler_params=pltpu.CompilerParams(vmem_limit_bytes=LIMIT),
        **specs,
    )


def oddness():
    return lax.rem(lax.axis_index("space"), 2)


def swapped(block):
    return jnp.swapaxes(block, 0, 1)


def bring_layer(loaded, out, x):
    zero = jnp.zeros((1, OWN, NZ), F32)
    out[x, 0:1] = zero
    out[x, NY + 1 : NY + 2] = zero
    for y in range(0, NY, 8):
        out[x, y + 1 : y + 9] = swapped(loaded[:, y : y + 8, :])


def pack_layer(layer, x, out, at):
    def rows(p, _):
        for r in range(4):
            two = layer[x, pl.ds(8 * p + 2 * r + 1, 2)].reshape(16, NZ)
            out[at + 4 * p + r] = two.astype(BF)
        return 0

    lax.fori_loop(0, NY // 8, rows, 0, unroll=True)


def pack_body(density, wind, out, old, loaded, sems):
    base = 2 - 2 * oddness()
    copies = [
        pltpu.make_async_copy(density.at[:, base + l], loaded.at[l], sems.at[l]) for l in range(2)
    ]
    for copy in copies:
        copy.start()
    for t in range(NY // 16):
        out[2 * HALF + t] = wind[0, 16 * t : 16 * t + 16, :]
    for l in range(2):
        copies[l].wait()
        bring_layer(loaded.at[l], old, l)
        pack_layer(old, l, out, l * HALF)


def block_pairs():
    for g in range(5):
        for q in range(4 if g == 4 else 8):
            yield g, 8 * g + q, (36 + q if g == 4 else (64 - 8 * g + q) % S)


def table_body(kernel, target, breakup, table, rows):
    lane = lax.broadcasted_iota(jnp.int32, (S, NZ), 1)
    second = lane >= S
    column = jnp.where(second, lane - S, lane)

    def blocks(a):
        parts = [a[0:8]]
        for g in range(1, 5):
            count = 4 if g == 4 else 8
            other = 36 if g == 4 else 8 * (8 - g)
            moved = pltpu.roll(a, S + 8 * g, 1)[other : other + count]
            own = a[8 * g : 8 * g + count]
            parts.append(jnp.where(column[0:count] >= 8 * g, own, moved))
        return parts

    def store(at, a):
        for g, part in enumerate(blocks(a)):
            rows[at, 8 * g : 8 * g + part.shape[0], :] = part

    def twice(a):
        return jnp.concatenate([a, a], 1)

    rates = kernel[...].astype(BF).astype(F32)
    targets = target[...].astype(F32)
    j = blocks(column.astype(F32))
    i = blocks(lax.broadcasted_iota(jnp.int32, (S, NZ), 0).astype(F32))
    store(0, twice(targets))
    store(1, twice(jnp.transpose(targets)))
    for g, (one, two) in enumerate(zip(blocks(twice(rates)), blocks(twice(jnp.transpose(rates))))):
        rows[2, 8 * g : 8 * g + one.shape[0], :] = jnp.where(j[g] >= i[g], one, 0.0)
        rows[3, 8 * g : 8 * g + one.shape[0], :] = jnp.where(j[g] > i[g], two, 0.0)
    k = lax.broadcasted_iota(jnp.int32, (S, NZ), 0).astype(F32)
    for t in range(BLOCKS // 2):
        to, to_t, rate, rate_t = [
            jnp.where(second[0:1], rows[q, 2 * t + 1 : 2 * t + 2, :], rows[q, 2 * t : 2 * t + 1, :])
            for q in range(4)
        ]
        one = jnp.where(to == k, rate, 0.0) + jnp.where(to_t == k, rate_t, 0.0)
        table[0:S, t * NZ : (t + 1) * NZ] = one.astype(BF)
    table[S:, : BLOCKS * S] = jnp.zeros((S, BLOCKS * S), BF)
    table[0:S, BLOCKS * S :] = breakup[...]
    table[S:, BLOCKS * S :] = rates.astype(BF)


def spread_rows(rows):
    return jnp.broadcast_to(rows[:, None, :], (8, OWN, NZ))


def within(ten, u, constants):
    here, from_above, from_below, spread = constants
    c = ten[1:9]
    return (
        c * (here - jnp.abs(u))
        + pltpu.roll(c, NZ - 1, 2) * from_above
        + pltpu.roll(c, 1, 2) * from_below
        + (ten[0:8] + ten[2:10]) * spread
    )


def from_west_of(u, spread):
    return spread + jnp.maximum(u, 0.0)


def from_east_of(u, spread):
    return spread - jnp.minimum(u, 0.0)


def per_section(ref):
    row = lax.broadcasted_iota(jnp.int32, (OWN, OWN), 0)
    column = lax.broadcasted_iota(jnp.int32, (OWN, OWN), 1)
    spread = jnp.where(row == column, jnp.broadcast_to(ref[...], (OWN, OWN)), 0.0)
    return jnp.broadcast_to(jnp.sum(spread, axis=1, keepdims=True), (OWN, NZ))


def inner_body(
    settling, diffusion, density, kept, wind, kernel, target, breakup,
    old, field, reach, constants, table, mid, rows,
):
    table_body(kernel, target, breakup, table, rows)
    sink, spread = per_section(settling), per_section(diffusion)
    lane = lax.broadcasted_iota(jnp.int32, (OWN, NZ), 1)
    held = (
        1.0 - sink - 6.0 * spread,
        jnp.where(lane == NZ - 1, 0.0, sink + spread),
        jnp.where(lane == 0, 0.0, spread),
        spread,
    )
    for i in range(4):
        constants[i] = held[i]
    zero = jnp.zeros((1, OWN, NZ), F32)
    for x in range(LAYERS):
        mid[x, 0:1] = zero
        mid[x, NY + 1 : NY + 2] = zero

    rest = 2 * oddness()
    own = 2 - rest
    for l in range(2):
        old[own + l] = kept[l]
        bring_layer(density.at[:, rest + l], old, rest + l)

    def substep(ref, y, store, store_reach=None):
        for x in range(LAYERS):
            u = spread_rows(wind[x, pl.ds(y, 8), :])
            west, east = from_west_of(u, spread), from_east_of(u, spread)
            value = within(ref[x, pl.ds(y, 10)], u, held)
            if x > 0:
                value = value + ref[x - 1, pl.ds(y + 1, 8)] * west
            if x < LAYERS - 1:
                value = value + ref[x + 1, pl.ds(y + 1, 8)] * east
            store(x, value)
            if store_reach is not None:
                store_reach(x, west if x < 2 else east)

    def first(b, _):
        y = pl.multiple_of(8 * b, 8)

        def store(x, value):
            mid[x, pl.ds(y + 1, 8)] = value

        def store_reach(x, value):
            reach[x, pl.ds(y, 8)] = value

        substep(old, y, store, store_reach)
        return 0

    def second(b, _):
        y = pl.multiple_of(8 * b, 8)

        def store(x, value):
            field[x, pl.ds(y, 8)] = value

        substep(mid, y, store)
        return 0

    lax.fori_loop(0, NY // 8, first, 0, unroll=True)
    lax.fori_loop(0, NY // 8, second, 0, unroll=True)


def side_body(
    plain, slabs, message, wind, old, inner, reach, constants, *refs
):
    if plain:
        done, field, rounded, halo, change, beyond, far = refs
    else:
        field, rounded, halo, change, beyond = refs
    odd = oddness()
    side = odd if plain else 1 - odd
    edge = 3 * side
    next_layer = 1 + side
    sign = 1.0 - 2.0 * side.astype(F32)
    inside = (lax.axis_index("space") != side * (slabs - 1)).astype(F32)
    held = tuple(constants[i] for i in range(4))
    spread = held[3]
    zero = jnp.zeros((1, OWN, NZ), F32)
    for ref in (halo, change):
        ref[0:1] = zero
        ref[NY + 1 : NY + 2] = zero
    if plain:
        for t in range(LAYERS):
            rounded[t] = done[t]
        for y in range(0, NY, 16):
            for l, out, first in ((1 - side, halo, 1), (side, far, 0)):
                rows = [message[2 * s + l, y : y + 16, :].astype(F32)[None] for s in range(OWN)]
                rows = jnp.concatenate(rows, 0)
                out[y + first : y + first + 8] = swapped(rows[:, 0:8])
                out[y + first + 8 : y + first + 16] = swapped(rows[:, 8:16])
    else:
        for p in range(HALF):
            two = message[(1 - side) * HALF + p].astype(F32).reshape(2, OWN, NZ)
            halo[2 * p + 1 : 2 * p + 3] = two

    for b in range(NY // 8):
        y = 8 * b
        if plain:
            farther = far[y : y + 8]
            winds = message[2 * OWN + 1 - side, 16 * (b // 2) : 16 * (b // 2) + 16, :].astype(F32)
        else:
            farther = [
                message[side * HALF + 4 * b + h].astype(F32).reshape(2, OWN, NZ) for h in range(4)
            ]
            farther = jnp.concatenate(farther, 0)
            winds = message[2 * HALF + b // 2].astype(F32)
        u = spread_rows(winds[8 * (b % 2) : 8 * (b % 2) + 8])
        outward = sign * u
        ten = halo[y : y + 10]
        value = (
            within(ten, u, held)
            + farther * (spread + jnp.maximum(outward, 0.0))
            + old[edge, y + 1 : y + 9] * (spread - jnp.minimum(outward, 0.0))
        )
        beyond[y : y + 8] = value * inside
        change[y + 1 : y + 9] = ten[1:9] * reach[edge, y : y + 8]

    for b in range(NY // 8):
        y = 8 * b
        u = spread_rows(wind[edge, y : y + 8, :])
        ten = change[y : y + 10]
        outer = inner[edge, y : y + 8] + within(ten, u, held)
        outer = outer + beyond[y : y + 8] * reach[edge, y : y + 8]
        second = inner[next_layer, y : y + 8] + ten[1:9] * reach[next_layer, y : y + 8]
        for at, value in ((side, outer), (1 - side, second)):
            field[at, y : y + 8] = value
            for h in range(4):
                two = value[2 * h : 2 * h + 2].reshape(16, NZ)
                p = 4 * b + h
                slot = (LAYERS if plain else 0) + 2 * at + p // PAIRS
                rounded[slot, p % PAIRS] = two.astype(BF)


WIDE = 16


def kinetics_body(cells, table, out, wide, products):
    def step(q, _):
        parts = []
        for u in range(WIDE):
            x = cells[:, WIDE * q + u].astype(F32)
            parts += [x[:, 0:8, :].reshape(S, NZ), x[:, 8:16, :].reshape(S, NZ)]
        n = jnp.concatenate(parts, 1)
        wide[...] = n
        for b, (g, i, other) in enumerate(block_pairs()):
            n_i, n_other = wide[i : i + 1, :], wide[other : other + 1, :]
            rows = []
            for t in range(8):
                if t < g:
                    at = 8 * (t + 8 - g)
                    rows.append(n[at : at + 8] * n_other)
                else:
                    rows.append(n[8 * t : 8 * t + 8] * n_i)
            products[S * b : S * (b + 1), :] = jnp.concatenate(rows, 0).astype(BF)
        products[BLOCKS * S :, :] = n.astype(BF)
        sums = jnp.dot(table[...], products[...], preferred_element_type=F32)
        total = sums[0:S] - n * sums[S:]
        for u in range(WIDE):
            at = 2 * NZ * u
            a = total[:, at : at + NZ].reshape(8, OWN, NZ)
            b = total[:, at + NZ : at + 2 * NZ].reshape(8, OWN, NZ)
            out[:, WIDE * q + u] = jnp.concatenate([a, b], 1).astype(BF)
        return 0

    lax.fori_loop(0, PAIRS // WIDE, step, 0)


def finish_body(near, far, tendency, out, held, sems):
    odd = oddness()
    copies = []
    for slot in range(2 * LAYERS):
        x, first = slot // 2, slot % 2 * HALF
        field, at = (near, x) if x < 2 else (far, x - 2)
        place = at + 2 * (1 - odd) if x < 2 else at + 2 * odd
        for y in range(0, HALF, 8):
            change = [tendency[slot, y // 2 + r].astype(F32).reshape(2, OWN, NZ) for r in range(4)]
            value = field[at, first + y : first + y + 8] + STEP * jnp.concatenate(change, 0)
            held[slot, :, y : y + 8, :] = swapped(value)
        target = out.at[:, place, pl.ds(first, HALF)]
        copies.append(pltpu.make_async_copy(held.at[slot], target, sems.at[slot]))
        copies[slot].start()
    for copy in copies:
        copy.wait()


def per_device(density, wind_speed, settling, diffusion, breakup, coag_kernel, pair_target):
    slabs = lax.axis_size("space")
    odd = oddness()
    vmem = pl.BlockSpec(memory_space=pltpu.VMEM)
    hbm = pl.BlockSpec(memory_space=pltpu.HBM)
    message = jax.ShapeDtypeStruct((2 * HALF + NY // 16, 16, NZ), BF)
    block = jax.ShapeDtypeStruct((8, PAIRS, 16, NZ), BF)
    cells_f32 = jax.ShapeDtypeStruct((LAYERS, NY, OWN, NZ), F32)
    padded = (LAYERS, NY + 2, OWN, NZ)

    both = jnp.concatenate([density, wind_speed[None]], 0)
    to_other = lax.dynamic_slice_in_dim(both, 2 * odd, 2, 1).astype(BF).reshape(2 * OWN + 2, NY, NZ)
    to_other, density, wind_held, settling, diffusion, breakup, coag_kernel, pair_target = (
        lax.optimization_barrier(
            (to_other, density, wind_speed, settling, diffusion, breakup, coag_kernel, pair_target)
        )
    )
    other = lax.ppermute(to_other, "space", [(i, ((i + 1) ^ 1) - 1) for i in range(1, slabs - 1)])
    to_partner, kept = call(
        pack_body,
        (message, jax.ShapeDtypeStruct((2, NY + 2, OWN, NZ), F32)),
        scratch=(
            pltpu.VMEM((2, OWN, NY, NZ), F32),
            pltpu.SemaphoreType.DMA((2,)),
        ),
        in_specs=[hbm, vmem],
    )(density, jnp.where(odd == 0, wind_held[LAYERS - 1 :], wind_held[0:1]).astype(BF))
    partner = lax.ppermute(to_partner, "space", [(i, i ^ 1) for i in range(slabs)])
    old, inner, reach, constants, table = call(
        inner_body,
        (
            jax.ShapeDtypeStruct(padded, F32),
            cells_f32,
            cells_f32,
            jax.ShapeDtypeStruct((4, OWN, NZ), F32),
            jax.ShapeDtypeStruct((2 * S, DEPTH), BF),
        ),
        scratch=(pltpu.VMEM(padded, F32), pltpu.VMEM((4, BLOCKS, NZ), F32)),
    )(
        settling.reshape(1, OWN), diffusion.reshape(1, OWN), density, kept, wind_held,
        coag_kernel, pair_target, breakup,
    )
    half = jax.ShapeDtypeStruct((2, NY, OWN, NZ), F32)
    half_block = jax.ShapeDtypeStruct((4, PAIRS, 16, NZ), BF)
    row_block = (NY + 2, OWN, NZ)
    scratch = (pltpu.VMEM(row_block, F32), pltpu.VMEM(row_block, F32), pltpu.VMEM((NY, OWN, NZ), F32))
    rest = (wind_held, old, inner, reach, constants)
    near, near_rounded = call(
        functools.partial(side_body, False, slabs),
        (half, half_block),
        scratch=scratch,
    )(partner, *rest)
    far, rounded = call(
        functools.partial(side_body, True, slabs),
        (half, block),
        scratch=scratch + (pltpu.VMEM((NY, OWN, NZ), F32),),
    )(other, *rest, near_rounded)
    cells = lax.all_to_all(rounded, "sec", split_axis=0, concat_axis=0, tiled=True)
    width = 2 * NZ * WIDE
    tendency = call(
        kinetics_body,
        block,
        scratch=(pltpu.VMEM((S, width), F32), pltpu.VMEM((DEPTH, width), BF)),
    )(cells, table)
    returned = lax.all_to_all(tendency, "sec", split_axis=0, concat_axis=0, tiled=True)
    return call(
        finish_body,
        jax.ShapeDtypeStruct((OWN, LAYERS, NY, NZ), F32),
        scratch=(
            pltpu.VMEM((2 * LAYERS, OWN, HALF, NZ), F32),
            pltpu.SemaphoreType.DMA((2 * LAYERS,)),
        ),
        in_specs=[vmem, vmem, vmem],
        out_specs=hbm,
    )(near, far, returned)


def solution(mesh):
    in_specs = (
        P("sec", "space", None, None),
        P("space", None, None),
        P("sec"),
        P("sec"),
        P(),
        P(),
        P(),
    )
    out_specs = P("sec", "space", None, None)
    return jax.shard_map(
        per_device, mesh=mesh, in_specs=in_specs, out_specs=out_specs, check_vma=False
    )
```
